512 devices in a mesh: attn: 8 (over x, core), tp: 8 (over z), exp: 8 (over y).
Axes of the slice: x: 4, y: 8, z: 8, core: 2. Of those that a mesh axis runs over, the one named last changes fastest.
Arguments:
- queries: bfloat16 [1536, 3072], P(('attn', 'exp'), 'tp'), may hold values from -180 to 180
- key_cache: bfloat16 [1536, 8, 32, 128], P(('attn', 'exp'), 'tp'), may hold values from -6 to 6
- value_cache: bfloat16 [1536, 8, 32, 128], P(('attn', 'exp'), 'tp'), may hold values from -6 to 6
- new_key: bfloat16 [1536, 1024], P(('attn', 'exp'), 'tp'), may hold values from -8 to 8
- new_value: bfloat16 [1536, 1024], P(('attn', 'exp'), 'tp'), may hold values from -6 to 6
- lengths: int32 [1536], P(('attn', 'exp')), may hold values from 2 to 32, as said below
- residual: bfloat16 [1536, 3072], P(('attn', 'exp'), 'tp'), may hold values from -150 to 150
- norm_gain: float32 [3072], replicated, may hold values from 0.1 to 1.9
- routes: int32 [1536, 2], P(('attn', 'exp')), may hold values from 0 to 7, all different within a row; in each aligned block of 24 rows (0 to 23, 24 to 47, ...) at most 12 rows name the same one
- route_weights: float32 [1536, 2], P(('attn', 'exp')), may hold values from 0.1 to 1
- w_gate_up: bfloat16 [8, 3072, 2, 16384], P('exp', None, None, ('attn', 'tp')), may hold values from -0.109375 to 0.109375
- w_down: bfloat16 [8, 16384, 3072], P('exp', 'attn', 'tp'), may hold values from -0.046875 to 0.046875
Outputs:
- attn_out: bfloat16 [1536, 3072], P(('attn', 'exp'), 'tp')
- moe_out: bfloat16 [1536, 3072], P(('attn', 'exp'), 'tp')
The draws below stay inside these ranges and needn't reach their ends.
Inputs may be any that keep to these rules, and one draw needn't show every extreme that they name: `lengths`: at least 2; some row holds exactly 32. `routes`: each row names two different experts; in the rows of one attention replica (aligned blocks of 24 rows) no expert is named by more than 12 rows, and in some block an expert is named by exactly 12 rows.
All inputs are finite; a program needn't handle non-finite values.
Results may differ from the reference program's by a relative error of at most 0.022.
Values may be sent and summed in bfloat16 or wider, within the bound.
No kernel may reach another device: no remote copies, remote signals or barrier semaphores. Data moves between devices by JAX's collectives and lax.ppermute only.
A program may use at most 64 MiB of HBM per device.

```python
import math
import jax
import jax.numpy as jnp
import numpy as np
from jax import lax

HD = 128
KV = 8
HEADS = 24
D = 3072
FF = 16384
EXPERTS = 8
ROWS_REP = 24
CAP = 12
LMAX = 32
ROWS = 1536


def shared_keys(key):
    base_keys = jnp.clip(jax.random.normal(jax.random.fold_in(key, 101), (ROWS, KV, LMAX, HD), jnp.float32), -6.0, 6.0)
    return base_keys


def draw_key_cache(key, part):
    base_keys = shared_keys(key)
    return base_keys.astype(jnp.bfloat16)


def draw_queries(key, part):
    key = jax.random.fold_in(key, 2)
    query_heads = jnp.clip(jax.random.normal(key, (ROWS, KV, HEADS // KV, HD), jnp.float32), -6.0, 6.0)
    return query_heads.reshape(ROWS, HEADS * HD).astype(jnp.bfloat16)


def draw_lengths(key, part):
    key = jax.random.fold_in(key, 3)
    samples = jax.random.randint(key, (ROWS,), 2, LMAX + 1)
    longest = jax.random.randint(jax.random.fold_in(key, 4), (), 0, ROWS)
    return samples.at[longest].set(LMAX).astype(jnp.int32)


def draw_residual(key, part):
    key = jax.random.fold_in(key, 5)
    column_pos = jnp.arange(D, dtype=jnp.float32) / D
    column_scale = jnp.exp(math.log(10.0) * column_pos) * jax.random.uniform(jax.random.fold_in(key, 6), (D,), jnp.float32, 0.5, 1.0)
    row_scale = jnp.exp(jax.random.uniform(jax.random.fold_in(key, 7), (ROWS, 1), jnp.float32, 0.0, math.log(10.0)))
    samples = jnp.clip(jax.random.normal(key, (ROWS, D), jnp.float32), -6.0, 6.0)
    return (0.25 * samples * row_scale * column_scale[None, :]).astype(jnp.bfloat16)


def levels(rng, extent, pieces, least, largest):
    factor_of = 1.0
    for dim, parts in pieces:
        draws = jax.random.uniform(jax.random.fold_in(jax.random.fold_in(rng, 6), dim), (parts,), jnp.float32, least / len(pieces), largest / len(pieces))
        factor_of = factor_of * jnp.repeat(jnp.exp(draws), extent[dim] // parts).reshape((-1,) + (1,) * (len(extent) - 1 - dim))
    return factor_of


def assign_block(rng, own, number, rows, number_of, top, most, lean):
    ranking = jax.random.permutation(rng, number_of)
    packed, ordinary = load_shares(number_of, rows * top, most, lean, True), load_shares(number_of, rows * top, most, lean, False)
    places = jnp.arange(number_of)

    def named(sizes, turn):
        used = int((sizes > 0).sum())
        fixed = max(1, used // 4)
        shifted = fixed + (places - fixed + turn * (used - fixed)) % max(1, number_of - fixed)
        return jnp.zeros((number_of,), jnp.int32).at[ranking[jnp.where(places < fixed, places, shifted)]].set(jnp.asarray(sizes, jnp.int32))

    sizes = jnp.where(number % 4 == 0, named(packed, number // 4), named(ordinary, number - number // 4 - 1))
    mixed = jax.random.permutation(jax.random.fold_in(own, 3), number_of)
    giver, taker = mixed[0:number_of // 2 * 2:2], mixed[1:number_of // 2 * 2:2]
    slack = jnp.minimum(sizes[giver] - 1, most - sizes[taker]) // 2
    slack = jnp.where((giver == ranking[0]) | (taker == ranking[0]) | (sizes[taker] == 0), 0, jnp.maximum(slack, 0))
    shifted = jax.random.randint(jax.random.fold_in(own, 4), (number_of // 2,), 0, 1 << 20) % (slack + 1)
    sizes = sizes.at[giver].add(-shifted).at[taker].add(shifted)
    labels = jnp.searchsorted(jnp.cumsum(sizes), jnp.arange(rows * top), side="right").astype(jnp.int32)
    table = labels.reshape(top, rows).T
    table = table[jax.random.permutation(jax.random.fold_in(own, 1), rows)]
    turn = jax.random.randint(jax.random.fold_in(own, 2), (rows, 1), 0, top)
    return jnp.take_along_axis(table, (jnp.arange(top)[None, :] + turn) % top, axis=1)


def load_shares(number_of, total, most, skew, full):
    weights = [(1 << 20) // math.isqrt(standing ** skew) + 1 for standing in range(1, number_of + 1)]
    largest = most if full else min(most, max(-(-total // number_of), total * weights[0] // sum(weights)))
    least = 1 if total - largest >= number_of - 1 else 0
    holding, spare = [largest] + [least] * (number_of - 1), total - largest - least * (number_of - 1)
    while spare > 0:
        candidates = [i for i in range(1, number_of) if holding[i] < largest] or [i for i in range(1, number_of) if holding[i] < most]
        whole, budget = sum([weights[i] for i in candidates]), spare
        for i in candidates:
            more = min(most - holding[i], max(1, budget * weights[i] // whole), spare)
            holding[i] = holding[i] + more
            spare = spare - more
    return np.array(holding)


def bell_draw(stream_key, shape, width, reach, split=(), kind=jnp.bfloat16):
    entries = jax.random.normal(stream_key, shape, jnp.float32) * width
    if len(split) > 0:
        entries = levels(stream_key, shape, split, -0.22, 0.18) * entries
    return jnp.clip(entries, min=-reach, max=reach).astype(kind)


def setup_inputs(seed: int = 0) -> dict:
    splits = jax.random.split(jax.random.key(seed), 13)
    queries = draw_queries(jax.random.fold_in(splits[12], 71), 0)
    key_cache = draw_key_cache(jax.random.fold_in(splits[12], 71), 0)
    value_cache = bell_draw(splits[2], (ROWS, KV, LMAX, HD), 1.0, 6.0, ((0, 64), (1, 8)))
    new_key = bell_draw(splits[3], (ROWS, KV * HD), 2.0, 8.0, ((0, 64), (1, 8)))
    new_value = bell_draw(splits[4], (ROWS, KV * HD), 1.0, 6.0, ((0, 64), (1, 8)))
    lengths = draw_lengths(jax.random.fold_in(splits[12], 71), 0)
    residual = draw_residual(jax.random.fold_in(splits[12], 71), 0)
    norm_gain = jnp.clip(1.0 + 0.18 * jax.random.normal(splits[7], (D,), jnp.float32), 0.1, 1.9)
    routes_keys = jax.random.split(jax.random.fold_in(splits[8], 1), ROWS // ROWS_REP)
    routes_turns = jax.random.permutation(jax.random.fold_in(splits[8], 3), ROWS // ROWS_REP)
    routes = jax.vmap(lambda own, number: assign_block(jax.random.fold_in(splits[8], 2), own, number, ROWS_REP, EXPERTS, 2, CAP, 2))(routes_keys, routes_turns).reshape((ROWS, 2))
    route_weights = jnp.clip(0.1 + 0.9 * jax.random.uniform(splits[9], (ROWS, 2), jnp.float32) ** levels(splits[9], (ROWS, 2), ((0, 64),), -0.2, 0.2), 0.1, 1.0)
    w_gate_up = bell_draw(splits[10], (EXPERTS, D, 2, FF), D ** -0.5, 0.109375, ((0, 8), (3, 64)))
    w_down = bell_draw(splits[11], (EXPERTS, FF, D), FF ** -0.5, 0.046875, ((0, 8), (1, 8), (2, 8)))
    return {"queries": queries, "key_cache": key_cache, "value_cache": value_cache, "new_key": new_key, "new_value": new_value, "lengths": lengths, "residual": residual, "norm_gain": norm_gain, "routes": routes, "route_weights": route_weights, "w_gate_up": w_gate_up, "w_down": w_down}


def attend(queries, key_cache, value_cache, new_key, new_value, lengths):
    row_count = queries.shape[0]
    query_heads = queries.astype(jnp.float32).reshape(row_count, KV, HEADS // KV, HD)
    fresh_key = new_key.astype(jnp.float32).reshape(row_count, KV, HD)
    fresh_value = new_value.astype(jnp.float32).reshape(row_count, KV, HD)
    score_scale = 1.0 / math.sqrt(HD)
    scores = jnp.einsum('rkgd,rkpd->rkgp', query_heads, key_cache.astype(jnp.float32)) * score_scale
    own_score = jnp.einsum('rkgd,rkd->rkg', query_heads, fresh_key) * score_scale
    valid = jnp.arange(LMAX, dtype=jnp.int32)[None, None, None, :] < lengths[:, None, None, None]
    masked = jnp.where(valid, scores, -jnp.inf)
    row_max = jnp.maximum(lax.optimization_barrier(jnp.max(masked, axis=-1)), own_score)
    exp_terms = jnp.exp(masked - row_max[..., None])
    own_term = jnp.exp(own_score - row_max)
    denominator = lax.optimization_barrier(jnp.sum(exp_terms, axis=-1)) + own_term
    probs = (exp_terms / denominator[..., None]).astype(jnp.bfloat16)
    probs_new = (own_term / denominator).astype(jnp.bfloat16)
    attended = jnp.einsum('rkgp,rkpd->rkgd', probs.astype(jnp.float32), value_cache.astype(jnp.float32))
    attended = attended + probs_new.astype(jnp.float32)[..., None] * fresh_value[:, :, None, :]
    return attended.reshape(row_count, HEADS * HD).astype(jnp.bfloat16)

def slots_of(block_routes):
    flat_routes = block_routes.reshape(-1)
    onehot = (flat_routes[:, None] == jnp.arange(EXPERTS, dtype=jnp.int32)[None, :]).astype(jnp.int32)
    before = jnp.cumsum(onehot, axis=0) - onehot
    return lax.optimization_barrier(jnp.sum(before * onehot, axis=1)).reshape(block_routes.shape).astype(jnp.int32)

def reference(queries, key_cache, value_cache, new_key, new_value, lengths, residual, norm_gain, routes, route_weights, w_gate_up, w_down):
    attn_out = attend(queries, key_cache, value_cache, new_key, new_value, lengths)
    hidden = (residual.astype(jnp.float32) + attn_out.astype(jnp.float32)).astype(jnp.bfloat16)
    hidden_wide = hidden.astype(jnp.float32)
    inv_rms = lax.rsqrt(lax.optimization_barrier(jnp.mean(hidden_wide * hidden_wide, axis=1, keepdims=True)) + 1e-05)
    normed = (hidden_wide * inv_rms * norm_gain[None, :]).astype(jnp.bfloat16)
    row_count = queries.shape[0]
    block_count = row_count // ROWS_REP
    slot_index = jax.vmap(slots_of)(routes.reshape(block_count, ROWS_REP, 2)).reshape(row_count, 2)
    block_of = jnp.arange(row_count, dtype=jnp.int32) // ROWS_REP
    position = (block_of[:, None] * CAP + slot_index).astype(jnp.int32)
    slot_total = block_count * CAP
    source_rows = jnp.repeat(normed, 2, axis=0)

    def run_expert(expert):
        destination = jnp.where(routes == expert, position, slot_total).reshape(-1).astype(jnp.int32)
        buffer = jnp.zeros((slot_total + 1, D), jnp.bfloat16).at[destination].set(source_rows)[:slot_total]
        gate_up = w_gate_up[expert].reshape(D, 2 * FF)
        pre_act = jnp.dot(buffer, gate_up, preferred_element_type=jnp.float32)
        unit_values = (jax.nn.silu(pre_act[:, :FF]) * pre_act[:, FF:]).astype(jnp.bfloat16)
        return jnp.dot(unit_values, w_down[expert], preferred_element_type=jnp.float32).astype(jnp.bfloat16)
    outputs = lax.map(run_expert, jnp.arange(EXPERTS, dtype=jnp.int32))
    picked = outputs[routes, position].astype(jnp.float32)
    moe_out = lax.optimization_barrier(jnp.sum(picked * route_weights[:, :, None], axis=1)).astype(jnp.bfloat16)
    return (attn_out, moe_out)
```

```python
import math

import jax
import jax.numpy as jnp
from jax import lax
from jax.experimental import pallas as pl
from jax.experimental.pallas import tpu as pltpu
from jax.sharding import Mesh, PartitionSpec as P

HD = 128
EXPERTS = 8


def attend_local(queries, key_cache, value_cache, new_key, new_value, lengths):
    row_count = key_cache.shape[0]
    kv_local = key_cache.shape[1]
    query_heads = queries.reshape(row_count, kv_local, -1, HD)
    fresh_key = new_key.reshape(row_count, kv_local, HD)
    fresh_value = new_value.reshape(row_count, kv_local, HD)
    score_scale = 1.0 / math.sqrt(HD)
    scores = (
        jnp.einsum("rkgd,rkpd->rkgp", query_heads, key_cache, preferred_element_type=jnp.float32)
        * score_scale
    )
    own_score = (
        jnp.einsum("rkgd,rkd->rkg", query_heads, fresh_key, preferred_element_type=jnp.float32)
        * score_scale
    )
    valid = (
        jnp.arange(key_cache.shape[2], dtype=jnp.int32)[None, None, None, :]
        < lengths[:, None, None, None]
    )
    masked = jnp.where(valid, scores, -jnp.inf)
    row_max = jnp.maximum(jnp.max(masked, axis=-1), own_score)
    exp_terms = jnp.exp(masked - row_max[..., None])
    own_term = jnp.exp(own_score - row_max)
    denominator = jnp.sum(exp_terms, axis=-1) + own_term
    probs = (exp_terms / denominator[..., None]).astype(jnp.bfloat16)
    probs_new = (own_term / denominator).astype(jnp.bfloat16)
    attended = jnp.einsum("rkgp,rkpd->rkgd", probs, value_cache, preferred_element_type=jnp.float32)
    attended = (
        attended
        + probs_new.astype(jnp.float32)[..., None] * fresh_value.astype(jnp.float32)[:, :, None, :]
    )
    return attended.reshape(row_count, -1).astype(jnp.bfloat16)


def slots_of(block_routes):
    flat_routes = block_routes.reshape(-1)
    onehot = (flat_routes[:, None] == jnp.arange(EXPERTS, dtype=jnp.int32)[None, :]).astype(
        jnp.int32
    )
    before = jnp.cumsum(onehot, axis=0) - onehot
    return jnp.sum(before * onehot, axis=1).reshape(block_routes.shape)


def shift(value, axis, step):
    size = lax.axis_size(axis)
    return lax.ppermute(value, axis, [(i, (i + step) % size) for i in range(size)])


def down_kernel(units_ref, own_ref, other_ref, out_ref, total_ref):
    step = pl.program_id(0)
    half = own_ref.shape[0]

    @pl.when(step == 0)
    def _():
        total_ref[...] = jnp.zeros_like(total_ref)

    total_ref[...] += jnp.dot(
        units_ref[0, :, :half], own_ref[...], preferred_element_type=jnp.float32
    ) + jnp.dot(units_ref[0, :, half:], other_ref[...], preferred_element_type=jnp.float32)

    @pl.when(step == pl.num_programs(0) - 1)
    def _():
        out_ref[...] = total_ref[...].astype(out_ref.dtype)


def down_project(units, own, other):
    groups, rows, width = units.shape
    half, cols = width // 2, own.shape[1]
    return pl.pallas_call(
        down_kernel,
        grid=(groups,),
        in_specs=[
            pl.BlockSpec((1, rows, width), lambda z: (z, 0, 0)),
            pl.BlockSpec((half, cols), lambda z: (z, 0)),
            pl.BlockSpec((half, cols), lambda z: (z, 0)),
        ],
        out_specs=pl.BlockSpec((rows, cols), lambda z: (0, 0)),
        out_shape=jax.ShapeDtypeStruct((rows, cols), jnp.bfloat16),
        scratch_shapes=[pltpu.VMEM((rows, cols), jnp.float32)],
        compiler_params=pltpu.CompilerParams(vmem_limit_bytes=24 * 1024 * 1024),
        cost_estimate=pl.CostEstimate(
            flops=2 * groups * rows * width * cols,
            bytes_accessed=2 * (groups * rows * width + 2 * own.size + rows * cols),
            transcendentals=0,
        ),
    )(units, own, other)


def body(
    queries,
    key_cache,
    value_cache,
    new_key,
    new_value,
    lengths,
    residual,
    norm_gain,
    routes,
    route_weights,
    w_gate_up,
    w_down,
):
    gate_up_own, down_own = w_gate_up[0], w_down[0]
    gate_up_other, down_other = shift(gate_up_own, "core", 1), shift(down_own, "core", 1)

    attn_out = attend_local(queries, key_cache, value_cache, new_key, new_value, lengths)
    hidden_part = (residual.astype(jnp.float32) + attn_out.astype(jnp.float32)).astype(jnp.bfloat16)
    n_x, n_tp, n_exp = lax.axis_size("x"), lax.axis_size("tp"), lax.axis_size("exp")
    row_count, part = hidden_part.shape
    copies = jnp.broadcast_to(hidden_part[None], (n_tp, row_count, part))
    hidden = lax.all_to_all(copies, "tp", split_axis=0, concat_axis=0, tiled=True)
    hidden_wide = hidden.astype(jnp.float32)
    feature_count = n_tp * part
    mean_square = jnp.sum(hidden_wide * hidden_wide, axis=(0, 2)) / feature_count
    inv_rms = lax.rsqrt(mean_square + 1e-05)
    gain = norm_gain.reshape(n_tp, 1, part)
    normed = (hidden_wide * inv_rms[None, :, None] * gain).astype(jnp.bfloat16)

    capacity = row_count // 2
    slot_total = EXPERTS * capacity
    target = routes * capacity + slots_of(routes)
    slot_ids = jnp.arange(slot_total, dtype=jnp.int32)
    placement = jnp.any(slot_ids[:, None, None] == target[None, :, :], axis=2).astype(jnp.bfloat16)
    normed = jnp.swapaxes(normed, 0, 1).reshape(row_count, feature_count)
    packed = jnp.dot(placement, normed, preferred_element_type=jnp.float32).astype(jnp.bfloat16)
    packed = packed.reshape(n_exp, capacity, feature_count)
    arrived = lax.all_to_all(packed, "exp", split_axis=0, concat_axis=0, tiled=True)
    own_rows = arrived.reshape(n_exp * capacity, feature_count)

    blocks = [own_rows] + [shift(own_rows, "x", k) for k in range(1, n_x)]
    rows = jnp.concatenate(blocks, axis=0)

    def units_of(weights):
        pre_act = jnp.einsum("rd,dgh->rgh", rows, weights, preferred_element_type=jnp.float32)
        return (jax.nn.silu(pre_act[:, 0]) * pre_act[:, 1]).astype(jnp.bfloat16)

    units = jnp.concatenate([units_of(gate_up_own), units_of(gate_up_other)], axis=1)
    gathered = lax.all_gather(units, "tp", axis=0, tiled=True)
    gathered = gathered.reshape(n_tp, units.shape[0], units.shape[1])
    partial = down_project(gathered, down_own, down_other)

    partial = partial.reshape(n_x, n_exp, capacity, part)
    x_index = lax.axis_index("x")
    order = (x_index - jnp.arange(n_x, dtype=jnp.int32)) % n_x
    partial = jnp.take(partial, order, axis=0)
    partial = partial.reshape(n_x * n_exp, capacity, part)
    returned = lax.all_to_all(partial, ("x", "exp"), split_axis=0, concat_axis=0, tiled=True)
    outputs = returned.reshape(n_x * slot_total, part)
    columns = slot_ids[None, :]
    picker = route_weights[:, 0:1] * (columns == target[:, 0:1]).astype(jnp.float32)
    picker = picker + route_weights[:, 1:2] * (columns == target[:, 1:2]).astype(jnp.float32)
    picker = jnp.tile(picker, (1, n_x))
    moe_out = jnp.dot(picker, outputs.astype(jnp.float32), precision=lax.Precision.HIGHEST).astype(
        jnp.bfloat16
    )
    return (attn_out, moe_out)


def solution(mesh):
    sizes = mesh.shape
    cores = 2
    chips = Mesh(
        mesh.devices.reshape(sizes["attn"] // cores, cores, sizes["tp"], sizes["exp"]),
        ("x", "core", "tp", "exp"),
    )
    rows = ("x", "core", "exp")
    return jax.shard_map(
        body,
        mesh=chips,
        in_specs=(
            P(rows, "tp"),
            P(rows, "tp", None, None),
            P(rows, "tp", None, None),
            P(rows, "tp"),
            P(rows, "tp"),
            P(rows),
            P(rows, "tp"),
            P(),
            P(rows, None),
            P(rows, None),
            P("exp", None, None, ("x", "core", "tp")),
            P("exp", ("x", "core"), "tp"),
        ),
        out_specs=(P(rows, "tp"), P(rows, "tp")),
        check_vma=False,
    )
```

```python
import functools
import math

import jax
import jax.numpy as jnp
from jax import lax
from jax.experimental import pallas as pl
from jax.experimental.pallas import tpu as pltpu
from jax.sharding import Mesh, PartitionSpec as P

HD = 128
EXPERTS = 8


def front_kernel(*refs):
    sources, (attn_ref, packed_ref, picker_ref), scratch = refs[:9], refs[9:12], refs[12:]
    landed, (query_rows, key_rows, value_rows, attended_rows, packed_rows, sems) = (
        scratch[:9],
        scratch[9:],
    )
    copies = [
        pltpu.make_async_copy(source, place, sems.at[index])
        for index, (source, place) in enumerate(zip(sources, landed))
    ]
    for copy in copies:
        copy.start()

    lengths_ref, routes_ref, route_weights_ref = landed[:3]
    for copy in copies[:3]:
        copy.wait()
    copy_count, experts, capacity, _ = packed_ref.shape
    row_count = routes_ref.shape[1]
    routes = routes_ref[...]
    expert_ids = lax.broadcasted_iota(jnp.int32, (experts, row_count), 0)
    first = (routes[0:1] == expert_ids).astype(jnp.float32)
    second = (routes[1:2] == expert_ids).astype(jnp.float32)
    row_ids = lax.broadcasted_iota(jnp.int32, (row_count, row_count), 0)
    later = row_ids < lax.broadcasted_iota(jnp.int32, (row_count, row_count), 1)
    before = jnp.dot(first + second, later.astype(jnp.float32), preferred_element_type=jnp.float32)
    slots = [
        jnp.sum(before * first, axis=0, keepdims=True),
        jnp.sum((before + first) * second, axis=0, keepdims=True),
    ]
    slot_total = experts * capacity
    slot_ids = lax.broadcasted_iota(jnp.int32, (slot_total, row_count), 0)
    placement = jnp.zeros(slot_ids.shape, jnp.float32)
    picker = jnp.zeros(slot_ids.shape, jnp.float32)
    for k in range(2):
        target = routes[k : k + 1] * capacity + slots[k].astype(jnp.int32)
        chosen = (slot_ids == target).astype(jnp.float32)
        placement = placement + chosen
        picker = picker + route_weights_ref[k : k + 1] * chosen
    for copy in range(copy_count):
        picker_ref[copy * slot_total : (copy + 1) * slot_total] = picker

    for copy in copies[3:]:
        copy.wait()
    queries_ref, new_key_ref, new_value_ref, residual_ref, keys_ref, values_ref = landed[3:]
    cached = keys_ref.shape[2]
    heads = queries_ref.shape[1] // HD
    query_rows[...] = queries_ref[...].astype(jnp.float32)
    key_rows[...] = new_key_ref[...].astype(jnp.float32)
    value_rows[...] = new_value_ref[...].astype(jnp.float32)
    score_scale = 1.0 / math.sqrt(HD)
    position = lax.broadcasted_iota(jnp.int32, (cached, 1), 0)
    for row in range(row_count):
        keys = keys_ref[row, 0].astype(jnp.float32)
        values = values_ref[row, 0].astype(jnp.float32)
        fresh_key, fresh_value = key_rows[row : row + 1], value_rows[row : row + 1]
        valid = position < lengths_ref[row]
        for head in range(heads):
            place = slice(head * HD, (head + 1) * HD)
            query = query_rows[row : row + 1, place]
            scores = jnp.sum(query * keys, axis=1, keepdims=True) * score_scale
            own_score = jnp.sum(query * fresh_key, axis=1, keepdims=True) * score_scale
            masked = jnp.where(valid, scores, -jnp.inf)
            row_max = jnp.maximum(jnp.max(masked, axis=0, keepdims=True), own_score)
            exp_terms = jnp.exp(masked - row_max)
            own_term = jnp.exp(own_score - row_max)
            denominator = jnp.sum(exp_terms, axis=0, keepdims=True) + own_term
            probs = (exp_terms / denominator).astype(jnp.bfloat16).astype(jnp.float32)
            probs_new = (own_term / denominator).astype(jnp.bfloat16).astype(jnp.float32)
            attended = jnp.sum(probs * values, axis=0, keepdims=True) + probs_new * fresh_value
            attended_rows[row : row + 1, place] = attended
    attn_out = attended_rows[...].astype(jnp.bfloat16)
    attn_ref[...] = attn_out
    hidden = residual_ref[...].astype(jnp.float32) + attn_out.astype(jnp.float32)
    packed_rows[...] = jnp.dot(
        placement.astype(jnp.bfloat16),
        hidden.astype(jnp.bfloat16),
        preferred_element_type=jnp.float32,
    )
    for expert in range(experts):
        rows = packed_rows[pl.ds(expert * capacity, capacity)].astype(jnp.bfloat16)
        for copy in range(copy_count):
            packed_ref[copy, expert] = rows


def attend_and_pack(lengths, routes, route_weights, tensors, copy_count):
    row_count, part = tensors[0].shape
    capacity = row_count // 2
    slot_total = EXPERTS * capacity
    tensors = [lengths, routes, route_weights] + tensors
    tensors = [pltpu.with_memory_space_constraint(value, pltpu.HBM) for value in tensors]
    rows = pltpu.VMEM((row_count, part), jnp.float32)
    narrow = pltpu.VMEM((row_count, HD), jnp.float32)
    vmem = pl.BlockSpec(memory_space=pltpu.VMEM)
    return pl.pallas_call(
        front_kernel,
        in_specs=[pl.BlockSpec(memory_space=pltpu.HBM)] * len(tensors),
        out_specs=[vmem] * 3,
        out_shape=[
            jax.ShapeDtypeStruct((row_count, part), jnp.bfloat16),
            jax.ShapeDtypeStruct((copy_count, EXPERTS, capacity, part), jnp.bfloat16),
            jax.ShapeDtypeStruct((copy_count * slot_total, row_count), jnp.float32),
        ],
        scratch_shapes=[pltpu.SMEM(lengths.shape, lengths.dtype)]
        + [pltpu.VMEM(value.shape, value.dtype) for value in tensors[1:]]
        + [
            rows,
            narrow,
            narrow,
            rows,
            pltpu.VMEM((slot_total, part), jnp.float32),
            pltpu.SemaphoreType.DMA((len(tensors),)),
        ],
        compiler_params=pltpu.CompilerParams(vmem_limit_bytes=24 * 1024 * 1024),
    )(*tensors)


def shift(value, axis, step):
    size = lax.axis_size(axis)
    return lax.ppermute(value, axis, [(i, (i + step) % size) for i in range(size)])


def fetch(sources, places, scratch, sems):
    width = scratch[0].shape[-2]
    copies = []
    for index, target in enumerate(scratch):
        part = pl.ds(pl.multiple_of(places[index] * width, width), width)
        group = []
        for source, ref in enumerate(sources):
            rows = ref.at[:, part] if len(ref.shape) == 3 else ref.at[part]
            group.append(pltpu.make_async_copy(rows, target.at[source], sems.at[index, source]))
            group[-1].start()
        copies.append(group)
    return copies


def up_products(place, gain_ref, row_ref, weights, total, squares):
    depth = row_ref.shape[1]
    part = pl.ds(pl.multiple_of(place * depth, depth), depth)
    rows = row_ref[...].astype(jnp.float32)
    square = rows * rows
    square = sum(square[:, lane : lane + HD] for lane in range(0, depth, HD))
    scaled = (rows * gain_ref[:, part]).astype(jnp.bfloat16)
    products = [
        jnp.dot(scaled, weights[index // 2, index % 2], preferred_element_type=jnp.float32)
        for index in range(4)
    ]
    if total is None:
        return products, square
    return [old + new for old, new in zip(total, products)], squares + square


def up_first_kernel(count, place_ref, gain_ref, own_ref, other_ref, *refs):
    row_refs, (total_ref, squares_ref, ahead_ref, weights, sems) = refs[:count], refs[-5:]
    scratch = [weights.at[index] for index in range(count)] + [ahead_ref]
    copies = fetch((own_ref, other_ref), place_ref, scratch, sems)
    total = squares = None
    for index, row_ref in enumerate(row_refs):
        for copy in copies[index]:
            copy.wait()
        total, squares = up_products(
            place_ref[index], gain_ref, row_ref, weights.at[index], total, squares
        )
    for index in range(4):
        total_ref[index] = total[index]
    squares_ref[...] = squares
    for copy in copies[count]:
        copy.wait()


def up_last_kernel(place_ref, gain_ref, row_ref, so_far_ref, squares_ref, weights_ref, out_ref):
    width = weights_ref.shape[3]
    features = gain_ref.shape[1]
    place = place_ref[place_ref.shape[0] - 1]
    so_far = [so_far_ref[index] for index in range(4)]
    total, squares = up_products(
        place, gain_ref, row_ref, weights_ref, so_far, squares_ref[...]
    )
    inv_rms = lax.rsqrt(jnp.sum(squares, axis=1, keepdims=True) / features + 1e-05)
    for index in range(2):
        gate, up = total[2 * index] * inv_rms, total[2 * index + 1] * inv_rms
        units = gate / (1.0 + jnp.exp(-gate)) * up
        out_ref[:, index * width : (index + 1) * width] = units.astype(out_ref.dtype)


def down_products(unit_ref, weights, total):
    half = unit_ref.shape[1] // 2
    for source in range(2):
        units = unit_ref[:, source * half : (source + 1) * half]
        product = jnp.dot(units, weights[source], preferred_element_type=jnp.float32)
        total = product if total is None else total + product
    return total


def down_first_kernel(count, place_ref, own_ref, other_ref, *refs):
    unit_refs, (total_ref, ahead_ref, weights, sems) = refs[:count], refs[-4:]
    scratch = [weights.at[index] for index in range(count)] + [ahead_ref]
    copies = fetch((own_ref, other_ref), place_ref, scratch, sems)
    total = None
    for index, unit_ref in enumerate(unit_refs):
        for copy in copies[index]:
            copy.wait()
        total = down_products(unit_ref, weights.at[index], total)
    total_ref[...] = total
    for copy in copies[count]:
        copy.wait()


def down_last_kernel(unit_ref, so_far_ref, weights_ref, out_ref, total_ref):
    total_ref[...] = down_products(unit_ref, weights_ref, so_far_ref[...])
    capacity = out_ref.shape[1]
    for block in range(out_ref.shape[0]):
        rows = pl.ds(block * capacity, capacity)
        out_ref[block] = total_ref[rows].astype(out_ref.dtype)


VMEM, HBM, SMEM = (
    pl.BlockSpec(memory_space=space) for space in (pltpu.VMEM, pltpu.HBM, pltpu.SMEM)
)
PARAMS = pltpu.CompilerParams(vmem_limit_bytes=24 * 1024 * 1024)


def cost(flops, bytes_accessed, transcendentals=0):
    return pl.CostEstimate(
        flops=flops, bytes_accessed=bytes_accessed, transcendentals=transcendentals
    )


def expert_units(blocks, places, gain, own, other):
    (rows, depth), width = blocks[0].shape, own.shape[2]
    own = pltpu.with_memory_space_constraint(own, pltpu.HBM)
    other = pltpu.with_memory_space_constraint(other, pltpu.HBM)
    *early, late = blocks
    count = len(early)
    weights = (2, 2, depth, width)
    sums = pl.pallas_call(
        functools.partial(up_first_kernel, count),
        in_specs=[SMEM, VMEM, HBM, HBM] + [VMEM] * count,
        out_specs=[VMEM] * 3,
        out_shape=[
            jax.ShapeDtypeStruct((4, rows, width), jnp.float32),
            jax.ShapeDtypeStruct((rows, HD), jnp.float32),
            jax.ShapeDtypeStruct(weights, jnp.bfloat16),
        ],
        scratch_shapes=[
            pltpu.VMEM((count,) + weights, jnp.bfloat16),
            pltpu.SemaphoreType.DMA((count + 1, 2)),
        ],
        compiler_params=PARAMS,
        cost_estimate=cost(8 * count * rows * depth * width, 8 * count * depth * width),
    )(places, gain, own, other, *early)
    return pl.pallas_call(
        up_last_kernel,
        in_specs=[SMEM] + [VMEM] * 5,
        out_specs=VMEM,
        out_shape=jax.ShapeDtypeStruct((rows, 2 * width), jnp.bfloat16),
        compiler_params=PARAMS,
        cost_estimate=cost(8 * rows * depth * width, 8 * depth * width, 2 * rows * width),
    )(places, gain, late, *sums)


def expert_outputs(blocks, places, own, other, shape):
    (rows, width), cols = blocks[0].shape, own.shape[1]
    own = pltpu.with_memory_space_constraint(own, pltpu.HBM)
    other = pltpu.with_memory_space_constraint(other, pltpu.HBM)
    *early, late = blocks
    count = len(early)
    weights = (2, width // 2, cols)
    sums = pl.pallas_call(
        functools.partial(down_first_kernel, count),
        in_specs=[SMEM, HBM, HBM] + [VMEM] * count,
        out_specs=[VMEM] * 2,
        out_shape=[
            jax.ShapeDtypeStruct((rows, cols), jnp.float32),
            jax.ShapeDtypeStruct(weights, jnp.bfloat16),
        ],
        scratch_shapes=[
            pltpu.VMEM((count,) + weights, jnp.bfloat16),
            pltpu.SemaphoreType.DMA((count + 1, 2)),
        ],
        compiler_params=PARAMS,
        cost_estimate=cost(2 * count * rows * width * cols, 2 * count * width * (rows + cols)),
    )(places, own, other, *early)
    return pl.pallas_call(
        down_last_kernel,
        in_specs=[VMEM] * 3,
        out_specs=VMEM,
        out_shape=jax.ShapeDtypeStruct(shape, jnp.bfloat16),
        scratch_shapes=[pltpu.VMEM((rows, cols), jnp.float32)],
        compiler_params=PARAMS,
        cost_estimate=cost(2 * rows * width * cols, 2 * width * (rows + cols)),
    )(late, *sums)


def around(block, axis):
    size = lax.axis_size(axis)
    before, after, blocks = block, block, [block]
    for distance in range(1, size // 2 + 1):
        before = shift(before, axis, 1)
        blocks.append(before)
        if distance < size - distance:
            after = shift(after, axis, size - 1)
            blocks.append(after)
    return blocks


def body(
    queries,
    key_cache,
    value_cache,
    new_key,
    new_value,
    lengths,
    residual,
    norm_gain,
    routes,
    route_weights,
    w_gate_up,
    w_down,
):
    n_x, n_tp, n_exp = lax.axis_size("x"), lax.axis_size("tp"), lax.axis_size("exp")

    attn_out, packed, picker = attend_and_pack(
        lengths,
        routes.T,
        route_weights.T,
        [queries, new_key, new_value, residual, key_cache, value_cache],
        n_x,
    )
    _, _, capacity, part = packed.shape
    packed = packed.reshape(n_x * n_exp, capacity, part)
    packed, w_gate_up, w_down = lax.optimization_barrier((packed, w_gate_up, w_down))
    gate_up_own, down_own = jnp.moveaxis(w_gate_up[0], 1, 0), w_down[0]
    gate_up_other, down_other = shift(gate_up_own, "core", 1), shift(down_own, "core", 1)
    arrived = lax.all_to_all(packed, ("x", "exp"), split_axis=0, concat_axis=0, tiled=True)
    arrived = arrived.reshape(n_x * n_exp * capacity, part)

    distance = jnp.array([0, -1, 1, -2, 2, -3, 3, 4], jnp.int32)
    places = (lax.axis_index("tp") + distance) % n_tp
    blocks = around(arrived, "tp")
    units = expert_units(blocks, places, norm_gain[None, :], gate_up_own, gate_up_other)
    blocks = around(units, "tp")
    shape = (n_x * n_exp, capacity, part)
    partial = expert_outputs(blocks, places, down_own, down_other, shape)

    returned = lax.all_to_all(partial, ("x", "exp"), split_axis=0, concat_axis=0, tiled=True)
    outputs = returned.reshape(n_x * n_exp * capacity, part).astype(jnp.float32)
    moe_out = lax.dot_general(
        picker, outputs, (((0,), (0,)), ((), ())), precision=lax.Precision.HIGHEST
    ).astype(jnp.bfloat16)
    return (attn_out, moe_out)


def solution(mesh):
    sizes = mesh.shape
    cores = 2
    chips = Mesh(
        mesh.devices.reshape(sizes["attn"] // cores, cores, sizes["tp"], sizes["exp"]),
        ("x", "core", "tp", "exp"),
    )
    rows = ("x", "core", "exp")
    return jax.shard_map(
        body,
        mesh=chips,
        in_specs=(
            P(rows, "tp"),
            P(rows, "tp", None, None),
            P(rows, "tp", None, None),
            P(rows, "tp"),
            P(rows, "tp"),
            P(rows),
            P(rows, "tp"),
            P(),
            P(rows, None),
            P(rows, None),
            P("exp", None, None, ("x", "core", "tp")),
            P("exp", ("x", "core"), "tp"),
        ),
        out_specs=(P(rows, "tp"), P(rows, "tp")),
        check_vma=False,
    )
```

```python
import functools
import math

import jax
import jax.numpy as jnp
from jax import lax
from jax.experimental import pallas as pl
from jax.experimental.pallas import tpu as pltpu
from jax.sharding import Mesh, PartitionSpec as P

HD = 128
EXPERTS = 8


def front_kernel(*refs):
    sources, (attn_ref, packed_ref, picker_ref), scratch = refs[:9], refs[9:12], refs[12:]
    landed, (query_rows, key_rows, value_rows, attended_rows, packed_rows, sems) = (
        scratch[:9],
        scratch[9:],
    )
    copies = [
        pltpu.make_async_copy(source, place, sems.at[index])
        for index, (source, place) in enumerate(zip(sources, landed))
    ]
    for copy in copies:
        copy.start()

    lengths_ref, routes_ref, route_weights_ref = landed[:3]
    for copy in copies[:3]:
        copy.wait()
    copy_count, experts, capacity, _ = packed_ref.shape
    row_count = routes_ref.shape[1]
    routes = routes_ref[...]
    expert_ids = lax.broadcasted_iota(jnp.int32, (experts, row_count), 0)
    first = (routes[0:1] == expert_ids).astype(jnp.float32)
    second = (routes[1:2] == expert_ids).astype(jnp.float32)
    row_ids = lax.broadcasted_iota(jnp.int32, (row_count, row_count), 0)
    later = row_ids < lax.broadcasted_iota(jnp.int32, (row_count, row_count), 1)
    before = jnp.dot(first + second, later.astype(jnp.float32), preferred_element_type=jnp.float32)
    slots = [
        jnp.sum(before * first, axis=0, keepdims=True),
        jnp.sum((before + first) * second, axis=0, keepdims=True),
    ]
    slot_total = experts * capacity
    slot_ids = lax.broadcasted_iota(jnp.int32, (slot_total, row_count), 0)
    placement = jnp.zeros(slot_ids.shape, jnp.float32)
    picker = jnp.zeros(slot_ids.shape, jnp.float32)
    for k in range(2):
        target = routes[k : k + 1] * capacity + slots[k].astype(jnp.int32)
        chosen = (slot_ids == target).astype(jnp.float32)
        placement = placement + chosen
        picker = picker + route_weights_ref[k : k + 1] * chosen
    for copy in range(copy_count):
        picker_ref[copy * slot_total : (copy + 1) * slot_total] = picker

    for copy in copies[3:]:
        copy.wait()
    queries_ref, new_key_ref, new_value_ref, residual_ref, keys_ref, values_ref = landed[3:]
    cached = keys_ref.shape[2]
    heads = queries_ref.shape[1] // HD
    query_rows[...] = queries_ref[...].astype(jnp.float32)
    key_rows[...] = new_key_ref[...].astype(jnp.float32)
    value_rows[...] = new_value_ref[...].astype(jnp.float32)
    score_scale = 1.0 / math.sqrt(HD)
    position = lax.broadcasted_iota(jnp.int32, (cached, 1), 0)
    for row in range(row_count):
        keys = keys_ref[row, 0].astype(jnp.float32)
        values = values_ref[row, 0].astype(jnp.float32)
        fresh_key, fresh_value = key_rows[row : row + 1], value_rows[row : row + 1]
        valid = position < lengths_ref[row]
        for head in range(heads):
            place = slice(head * HD, (head + 1) * HD)
            query = query_rows[row : row + 1, place]
            scores = jnp.sum(query * keys, axis=1, keepdims=True) * score_scale
            own_score = jnp.sum(query * fresh_key, axis=1, keepdims=True) * score_scale
            masked = jnp.where(valid, scores, -jnp.inf)
            row_max = jnp.maximum(jnp.max(masked, axis=0, keepdims=True), own_score)
            exp_terms = jnp.exp(masked - row_max)
            own_term = jnp.exp(own_score - row_max)
            denominator = jnp.sum(exp_terms, axis=0, keepdims=True) + own_term
            probs = (exp_terms / denominator).astype(jnp.bfloat16).astype(jnp.float32)
            probs_new = (own_term / denominator).astype(jnp.bfloat16).astype(jnp.float32)
            attended = jnp.sum(probs * values, axis=0, keepdims=True) + probs_new * fresh_value
            attended_rows[row : row + 1, place] = attended
    attn_out = attended_rows[...].astype(jnp.bfloat16)
    attn_ref[...] = attn_out
    hidden = residual_ref[...].astype(jnp.float32) + attn_out.astype(jnp.float32)
    packed_rows[...] = jnp.dot(
        placement.astype(jnp.bfloat16),
        hidden.astype(jnp.bfloat16),
        preferred_element_type=jnp.float32,
    )
    for expert in range(experts):
        rows = packed_rows[pl.ds(expert * capacity, capacity)].astype(jnp.bfloat16)
        for copy in range(copy_count):
            packed_ref[copy, expert] = rows


def attend_and_pack(lengths, routes, route_weights, tensors, copy_count):
    row_count, part = tensors[0].shape
    capacity = row_count // 2
    slot_total = EXPERTS * capacity
    tensors = [lengths, routes, route_weights] + tensors
    tensors = [pltpu.with_memory_space_constraint(value, pltpu.HBM) for value in tensors]
    rows = pltpu.VMEM((row_count, part), jnp.float32)
    narrow = pltpu.VMEM((row_count, HD), jnp.float32)
    vmem = pl.BlockSpec(memory_space=pltpu.VMEM)
    return pl.pallas_call(
        front_kernel,
        in_specs=[pl.BlockSpec(memory_space=pltpu.HBM)] * len(tensors),
        out_specs=[vmem] * 3,
        out_shape=[
            jax.ShapeDtypeStruct((row_count, part), jnp.bfloat16),
            jax.ShapeDtypeStruct((copy_count, EXPERTS, capacity, part), jnp.bfloat16),
            jax.ShapeDtypeStruct((copy_count * slot_total, row_count), jnp.float32),
        ],
        scratch_shapes=[pltpu.SMEM(lengths.shape, lengths.dtype)]
        + [pltpu.VMEM(value.shape, value.dtype) for value in tensors[1:]]
        + [
            rows,
            narrow,
            narrow,
            rows,
            pltpu.VMEM((slot_total, part), jnp.float32),
            pltpu.SemaphoreType.DMA((len(tensors),)),
        ],
        compiler_params=pltpu.CompilerParams(vmem_limit_bytes=24 * 1024 * 1024),
    )(*tensors)


def shift(value, axis, step):
    size = lax.axis_size(axis)
    return lax.ppermute(value, axis, [(i, (i + step) % size) for i in range(size)])


def fetch(sources, places, scratch, sems):
    width = scratch[0].shape[-2]
    copies = []
    for index, target in enumerate(scratch):
        part = pl.ds(pl.multiple_of(places[index] * width, width), width)
        group = []
        for source, ref in enumerate(sources):
            group.append(
                pltpu.make_async_copy(ref.at[part], target.at[source], sems.at[index, source])
            )
            group[-1].start()
        copies.append(group)
    return copies


def up_products(place, gain_ref, row_ref, weights, total, squares):
    depth = row_ref.shape[1]
    part = pl.ds(pl.multiple_of(place * depth, depth), depth)
    rows = row_ref[...].astype(jnp.float32)
    square = rows * rows
    square = sum(square[:, lane : lane + HD] for lane in range(0, depth, HD))
    scaled = (rows * gain_ref[:, part]).astype(jnp.bfloat16)
    products = [
        jnp.dot(scaled, weights[index], preferred_element_type=jnp.float32)
        for index in range(4)
    ]
    if total is None:
        return products, square
    return [old + new for old, new in zip(total, products)], squares + square


def up_first_kernel(count, place_ref, gain_ref, *refs):
    source_refs, row_refs = refs[:4], refs[4 : 4 + count]
    total_ref, squares_ref, ahead_ref, weights, sems = refs[-5:]
    scratch = [weights.at[index] for index in range(count)] + [ahead_ref]
    copies = fetch(source_refs, place_ref, scratch, sems)
    total = squares = None
    for index, row_ref in enumerate(row_refs):
        for copy in copies[index]:
            copy.wait()
        total, squares = up_products(
            place_ref[index], gain_ref, row_ref, weights.at[index], total, squares
        )
    for index in range(4):
        total_ref[index] = total[index]
    squares_ref[...] = squares
    for copy in copies[count]:
        copy.wait()


def up_last_kernel(place_ref, gain_ref, row_ref, so_far_ref, squares_ref, weights_ref, out_ref):
    width = weights_ref.shape[2]
    features = gain_ref.shape[1]
    place = place_ref[place_ref.shape[0] - 1]
    so_far = [so_far_ref[index] for index in range(4)]
    total, squares = up_products(
        place, gain_ref, row_ref, weights_ref, so_far, squares_ref[...]
    )
    inv_rms = lax.rsqrt(jnp.sum(squares, axis=1, keepdims=True) / features + 1e-05)
    for index in range(2):
        gate, up = total[2 * index] * inv_rms, total[2 * index + 1] * inv_rms
        units = gate / (1.0 + jnp.exp(-gate)) * up
        out_ref[:, index * width : (index + 1) * width] = units.astype(out_ref.dtype)


def down_products(unit_ref, weights, total):
    half = unit_ref.shape[1] // 2
    for source in range(2):
        units = unit_ref[:, source * half : (source + 1) * half]
        product = jnp.dot(units, weights[source], preferred_element_type=jnp.float32)
        total = product if total is None else total + product
    return total


def down_first_kernel(count, place_ref, own_ref, other_ref, *refs):
    unit_refs, (total_ref, ahead_ref, weights, sems) = refs[:count], refs[-4:]
    scratch = [weights.at[index] for index in range(count)] + [ahead_ref]
    copies = fetch((own_ref, other_ref), place_ref, scratch, sems)
    total = None
    for index, unit_ref in enumerate(unit_refs):
        for copy in copies[index]:
            copy.wait()
        total = down_products(unit_ref, weights.at[index], total)
    total_ref[...] = total
    for copy in copies[count]:
        copy.wait()


def down_last_kernel(unit_ref, so_far_ref, weights_ref, out_ref, total_ref):
    total_ref[...] = down_products(unit_ref, weights_ref, so_far_ref[...])
    capacity = out_ref.shape[1]
    for block in range(out_ref.shape[0]):
        rows = pl.ds(block * capacity, capacity)
        out_ref[block] = total_ref[rows].astype(out_ref.dtype)


VMEM, HBM, SMEM = (
    pl.BlockSpec(memory_space=space) for space in (pltpu.VMEM, pltpu.HBM, pltpu.SMEM)
)
PARAMS = pltpu.CompilerParams(vmem_limit_bytes=24 * 1024 * 1024)


def cost(flops, bytes_accessed, transcendentals=0):
    return pl.CostEstimate(
        flops=flops, bytes_accessed=bytes_accessed, transcendentals=transcendentals
    )


def expert_units(blocks, places, gain, sources):
    (rows, depth), width = blocks[0].shape, sources[0].shape[1]
    sources = [pltpu.with_memory_space_constraint(source, pltpu.HBM) for source in sources]
    *early, late = blocks
    count = len(early)
    weights = (4, depth, width)
    sums = pl.pallas_call(
        functools.partial(up_first_kernel, count),
        in_specs=[SMEM, VMEM] + [HBM] * 4 + [VMEM] * count,
        out_specs=[VMEM] * 3,
        out_shape=[
            jax.ShapeDtypeStruct((4, rows, width), jnp.float32),
            jax.ShapeDtypeStruct((rows, HD), jnp.float32),
            jax.ShapeDtypeStruct(weights, jnp.bfloat16),
        ],
        scratch_shapes=[
            pltpu.VMEM((count,) + weights, jnp.bfloat16),
            pltpu.SemaphoreType.DMA((count + 1, 4)),
        ],
        compiler_params=PARAMS,
        cost_estimate=cost(8 * count * rows * depth * width, 8 * count * depth * width),
    )(places, gain, *sources, *early)
    return pl.pallas_call(
        up_last_kernel,
        in_specs=[SMEM] + [VMEM] * 5,
        out_specs=VMEM,
        out_shape=jax.ShapeDtypeStruct((rows, 2 * width), jnp.bfloat16),
        compiler_params=PARAMS,
        cost_estimate=cost(8 * rows * depth * width, 8 * depth * width, 2 * rows * width),
    )(places, gain, late, *sums)


def expert_outputs(blocks, places, own, other, shape):
    (rows, width), cols = blocks[0].shape, own.shape[1]
    own = pltpu.with_memory_space_constraint(own, pltpu.HBM)
    other = pltpu.with_memory_space_constraint(other, pltpu.HBM)
    *early, late = blocks
    count = len(early)
    weights = (2, width // 2, cols)
    sums = pl.pallas_call(
        functools.partial(down_first_kernel, count),
        in_specs=[SMEM, HBM, HBM] + [VMEM] * count,
        out_specs=[VMEM] * 2,
        out_shape=[
            jax.ShapeDtypeStruct((rows, cols), jnp.float32),
            jax.ShapeDtypeStruct(weights, jnp.bfloat16),
        ],
        scratch_shapes=[
            pltpu.VMEM((count,) + weights, jnp.bfloat16),
            pltpu.SemaphoreType.DMA((count + 1, 2)),
        ],
        compiler_params=PARAMS,
        cost_estimate=cost(2 * count * rows * width * cols, 2 * count * width * (rows + cols)),
    )(places, own, other, *early)
    return pl.pallas_call(
        down_last_kernel,
        in_specs=[VMEM] * 3,
        out_specs=VMEM,
        out_shape=jax.ShapeDtypeStruct(shape, jnp.bfloat16),
        scratch_shapes=[pltpu.VMEM((rows, cols), jnp.float32)],
        compiler_params=PARAMS,
        cost_estimate=cost(2 * rows * width * cols, 2 * width * (rows + cols)),
    )(late, *sums)


def around(block, axis):
    size = lax.axis_size(axis)
    before, after, blocks = block, block, [block]
    for distance in range(1, size // 2 + 1):
        before = shift(before, axis, 1)
        blocks.append(before)
        if distance < size - distance:
            after = shift(after, axis, size - 1)
            blocks.append(after)
    return blocks


def body(
    queries,
    key_cache,
    value_cache,
    new_key,
    new_value,
    lengths,
    residual,
    norm_gain,
    routes,
    route_weights,
    w_gate_up,
    w_down,
):
    n_x, n_tp, n_exp = lax.axis_size("x"), lax.axis_size("tp"), lax.axis_size("exp")

    attn_out, packed, picker = attend_and_pack(
        lengths,
        routes.T,
        route_weights.T,
        [queries, new_key, new_value, residual, key_cache, value_cache],
        n_x,
    )
    _, _, capacity, part = packed.shape
    packed = packed.reshape(n_x * n_exp, capacity, part)
    packed, w_gate_up, w_down = lax.optimization_barrier((packed, w_gate_up, w_down))
    gate_own, up_own, down_own = w_gate_up[0, :, 0], w_gate_up[0, :, 1], w_down[0]
    gate_other, up_other, down_other = (
        shift(weights, "core", 1) for weights in (gate_own, up_own, down_own)
    )
    arrived = lax.all_to_all(packed, ("x", "exp"), split_axis=0, concat_axis=0, tiled=True)
    arrived = arrived.reshape(n_x * n_exp * capacity, part)

    distance = jnp.array([0, -1, 1, -2, 2, -3, 3, 4], jnp.int32)
    places = (lax.axis_index("tp") + distance) % n_tp
    blocks = around(arrived, "tp")
    sources = (gate_own, up_own, gate_other, up_other)
    units = expert_units(blocks, places, norm_gain[None, :], sources)
    blocks = around(units, "tp")
    shape = (n_x * n_exp, capacity, part)
    partial = expert_outputs(blocks, places, down_own, down_other, shape)

    returned = lax.all_to_all(partial, ("x", "exp"), split_axis=0, concat_axis=0, tiled=True)
    outputs = returned.reshape(n_x * n_exp * capacity, part).astype(jnp.float32)
    moe_out = lax.dot_general(
        picker, outputs, (((0,), (0,)), ((), ())), precision=lax.Precision.HIGHEST
    ).astype(jnp.bfloat16)
    return (attn_out, moe_out)


def solution(mesh):
    sizes = mesh.shape
    cores = 2
    chips = Mesh(
        mesh.devices.reshape(sizes["attn"] // cores, cores, sizes["tp"], sizes["exp"]),
        ("x", "core", "tp", "exp"),
    )
    rows = ("x", "core", "exp")
    return jax.shard_map(
        body,
        mesh=chips,
        in_specs=(
            P(rows, "tp"),
            P(rows, "tp", None, None),
            P(rows, "tp", None, None),
            P(rows, "tp"),
            P(rows, "tp"),
            P(rows),
            P(rows, "tp"),
            P(),
            P(rows, None),
            P(rows, None),
            P("exp", None, None, ("x", "core", "tp")),
            P("exp", ("x", "core"), "tp"),
        ),
        out_specs=(P(rows, "tp"), P(rows, "tp")),
        check_vma=False,
    )
```

```python
import functools
import math

import jax
import jax.numpy as jnp
from jax import lax
from jax.experimental import pallas as pl
from jax.experimental.pallas import tpu as pltpu
from jax.sharding import Mesh, PartitionSpec as P

HD = 128
EXPERTS = 8


def front_kernel(*refs):
    sources, (attn_ref, packed_ref, picker_ref), scratch = refs[:9], refs[9:12], refs[12:]
    landed, (query_rows, key_rows, value_rows, attended_rows, packed_rows, sems) = (
        scratch[:9],
        scratch[9:],
    )
    copies = [
        pltpu.make_async_copy(source, place, sems.at[index])
        for index, (source, place) in enumerate(zip(sources, landed))
    ]
    for copy in copies:
        copy.start()

    lengths_ref, routes_ref, route_weights_ref = landed[:3]
    for copy in copies[:3]:
        copy.wait()
    copy_count, experts, capacity, _ = packed_ref.shape
    row_count = routes_ref.shape[1]
    routes = routes_ref[...]
    expert_ids = lax.broadcasted_iota(jnp.int32, (experts, row_count), 0)
    first = (routes[0:1] == expert_ids).astype(jnp.float32)
    second = (routes[1:2] == expert_ids).astype(jnp.float32)
    row_ids = lax.broadcasted_iota(jnp.int32, (row_count, row_count), 0)
    later = row_ids < lax.broadcasted_iota(jnp.int32, (row_count, row_count), 1)
    before = jnp.dot(first + second, later.astype(jnp.float32), preferred_element_type=jnp.float32)
    slots = [
        jnp.sum(before * first, axis=0, keepdims=True),
        jnp.sum((before + first) * second, axis=0, keepdims=True),
    ]
    slot_total = experts * capacity
    slot_ids = lax.broadcasted_iota(jnp.int32, (slot_total, row_count), 0)
    placement = jnp.zeros(slot_ids.shape, jnp.float32)
    picker = jnp.zeros(slot_ids.shape, jnp.float32)
    for k in range(2):
        target = routes[k : k + 1] * capacity + slots[k].astype(jnp.int32)
        chosen = (slot_ids == target).astype(jnp.float32)
        placement = placement + chosen
        picker = picker + route_weights_ref[k : k + 1] * chosen
    picker_ref[...] = picker

    for copy in copies[3:]:
        copy.wait()
    queries_ref, new_key_ref, new_value_ref, residual_ref, keys_ref, values_ref = landed[3:]
    cached = keys_ref.shape[2]
    heads = queries_ref.shape[1] // HD
    query_rows[...] = queries_ref[...].astype(jnp.float32)
    key_rows[...] = new_key_ref[...].astype(jnp.float32)
    value_rows[...] = new_value_ref[...].astype(jnp.float32)
    score_scale = 1.0 / math.sqrt(HD)
    position = lax.broadcasted_iota(jnp.int32, (cached, 1), 0)
    for row in range(row_count):
        keys = keys_ref[row, 0].astype(jnp.float32)
        values = values_ref[row, 0].astype(jnp.float32)
        fresh_key, fresh_value = key_rows[row : row + 1], value_rows[row : row + 1]
        valid = position < lengths_ref[row]
        for head in range(heads):
            place = slice(head * HD, (head + 1) * HD)
            query = query_rows[row : row + 1, place]
            scores = jnp.sum(query * keys, axis=1, keepdims=True) * score_scale
            own_score = jnp.sum(query * fresh_key, axis=1, keepdims=True) * score_scale
            masked = jnp.where(valid, scores, -jnp.inf)
            row_max = jnp.maximum(jnp.max(masked, axis=0, keepdims=True), own_score)
            exp_terms = jnp.exp(masked - row_max)
            own_term = jnp.exp(own_score - row_max)
            denominator = jnp.sum(exp_terms, axis=0, keepdims=True) + own_term
            probs = (exp_terms / denominator).astype(jnp.bfloat16).astype(jnp.float32)
            probs_new = (own_term / denominator).astype(jnp.bfloat16).astype(jnp.float32)
            attended = jnp.sum(probs * values, axis=0, keepdims=True) + probs_new * fresh_value
            attended_rows[row : row + 1, place] = attended
    attn_out = attended_rows[...].astype(jnp.bfloat16)
    attn_ref[...] = attn_out
    hidden = residual_ref[...].astype(jnp.float32) + attn_out.astype(jnp.float32)
    packed_rows[...] = jnp.dot(
        placement.astype(jnp.bfloat16),
        hidden.astype(jnp.bfloat16),
        preferred_element_type=jnp.float32,
    )
    for expert in range(experts):
        rows = packed_rows[pl.ds(expert * capacity, capacity)].astype(jnp.bfloat16)
        for copy in range(copy_count):
            packed_ref[copy, expert] = rows


def attend_and_pack(lengths, routes, route_weights, tensors, copy_count):
    row_count, part = tensors[0].shape
    capacity = row_count // 2
    slot_total = EXPERTS * capacity
    tensors = [lengths, routes, route_weights] + tensors
    tensors = [pltpu.with_memory_space_constraint(value, pltpu.HBM) for value in tensors]
    rows = pltpu.VMEM((row_count, part), jnp.float32)
    narrow = pltpu.VMEM((row_count, HD), jnp.float32)
    vmem = pl.BlockSpec(memory_space=pltpu.VMEM)
    return pl.pallas_call(
        front_kernel,
        in_specs=[pl.BlockSpec(memory_space=pltpu.HBM)] * len(tensors),
        out_specs=[vmem] * 3,
        out_shape=[
            jax.ShapeDtypeStruct((row_count, part), jnp.bfloat16),
            jax.ShapeDtypeStruct((copy_count, EXPERTS, capacity, part), jnp.bfloat16),
            jax.ShapeDtypeStruct((slot_total, row_count), jnp.float32),
        ],
        scratch_shapes=[pltpu.SMEM(lengths.shape, lengths.dtype)]
        + [pltpu.VMEM(value.shape, value.dtype) for value in tensors[1:]]
        + [
            rows,
            narrow,
            narrow,
            rows,
            pltpu.VMEM((slot_total, part), jnp.float32),
            pltpu.SemaphoreType.DMA((len(tensors),)),
        ],
        compiler_params=pltpu.CompilerParams(vmem_limit_bytes=24 * 1024 * 1024),
    )(*tensors)


def shift(value, axis, step):
    size = lax.axis_size(axis)
    return lax.ppermute(value, axis, [(i, (i + step) % size) for i in range(size)])


def fetch(sources, places, scratch, sems):
    width = scratch[0].shape[-2]
    copies = []
    for index, target in enumerate(scratch):
        part = pl.ds(pl.multiple_of(places[index] * width, width), width)
        group = []
        for source, ref in enumerate(sources):
            group.append(
                pltpu.make_async_copy(ref.at[part], target.at[source], sems.at[index, source])
            )
            group[-1].start()
        copies.append(group)
    return copies


def up_products(place, gain_ref, row_ref, weights, total, squares):
    depth = row_ref.shape[1]
    part = pl.ds(pl.multiple_of(place * depth, depth), depth)
    rows = row_ref[...].astype(jnp.float32)
    square = rows * rows
    square = sum(square[:, lane : lane + HD] for lane in range(0, depth, HD))
    scaled = (rows * gain_ref[:, part]).astype(jnp.bfloat16)
    products = [
        jnp.dot(scaled, weights[index], preferred_element_type=jnp.float32)
        for index in range(4)
    ]
    if total is None:
        return products, square
    return [old + new for old, new in zip(total, products)], squares + square


def up_first_kernel(count, place_ref, gain_ref, *refs):
    source_refs, row_refs = refs[:4], refs[4 : 4 + count]
    total_ref, squares_ref, ahead_ref, weights, sems = refs[-5:]
    scratch = [weights.at[index] for index in range(count)] + [ahead_ref]
    copies = fetch(source_refs, place_ref, scratch, sems)
    total = squares = None
    for index, row_ref in enumerate(row_refs):
        for copy in copies[index]:
            copy.wait()
        total, squares = up_products(
            place_ref[index], gain_ref, row_ref, weights.at[index], total, squares
        )
    for index in range(4):
        total_ref[index] = total[index]
    squares_ref[...] = squares
    for copy in copies[count]:
        copy.wait()


def up_last_kernel(place_ref, gain_ref, row_ref, so_far_ref, squares_ref, weights_ref, out_ref):
    width = weights_ref.shape[2]
    features = gain_ref.shape[1]
    place = place_ref[place_ref.shape[0] - 1]
    so_far = [so_far_ref[index] for index in range(4)]
    total, squares = up_products(
        place, gain_ref, row_ref, weights_ref, so_far, squares_ref[...]
    )
    inv_rms = lax.rsqrt(jnp.sum(squares, axis=1, keepdims=True) / features + 1e-05)
    for index in range(2):
        gate, up = total[2 * index] * inv_rms, total[2 * index + 1] * inv_rms
        units = gate / (1.0 + jnp.exp(-gate)) * up
        out_ref[:, index * width : (index + 1) * width] = units.astype(out_ref.dtype)


def down_products(unit_ref, weights, total):
    half = unit_ref.shape[1] // 2
    for source in range(2):
        units = unit_ref[:, source * half : (source + 1) * half]
        product = jnp.dot(units, weights[source], preferred_element_type=jnp.float32)
        total = product if total is None else total + product
    return total


def down_first_kernel(count, place_ref, own_ref, other_ref, *refs):
    unit_refs, (total_ref, ahead_ref, weights, sems) = refs[:count], refs[-4:]
    scratch = [weights.at[index] for index in range(count)] + [ahead_ref]
    copies = fetch((own_ref, other_ref), place_ref, scratch, sems)
    total = None
    for index, unit_ref in enumerate(unit_refs):
        for copy in copies[index]:
            copy.wait()
        total = down_products(unit_ref, weights.at[index], total)
    total_ref[...] = total
    for copy in copies[count]:
        copy.wait()


def down_last_kernel(unit_ref, so_far_ref, weights_ref, out_ref, total_ref):
    total_ref[...] = down_products(unit_ref, weights_ref, so_far_ref[...])
    capacity = out_ref.shape[1]
    for block in range(out_ref.shape[0]):
        rows = pl.ds(block * capacity, capacity)
        out_ref[block] = total_ref[rows].astype(out_ref.dtype)


VMEM, HBM, SMEM = (
    pl.BlockSpec(memory_space=space) for space in (pltpu.VMEM, pltpu.HBM, pltpu.SMEM)
)
PARAMS = pltpu.CompilerParams(vmem_limit_bytes=24 * 1024 * 1024)


def cost(flops, bytes_accessed, transcendentals=0):
    return pl.CostEstimate(
        flops=flops, bytes_accessed=bytes_accessed, transcendentals=transcendentals
    )


def expert_units(blocks, places, gain, sources):
    (rows, depth), width = blocks[0].shape, sources[0].shape[1]
    sources = [pltpu.with_memory_space_constraint(source, pltpu.HBM) for source in sources]
    *early, late = blocks
    count = len(early)
    weights = (4, depth, width)
    sums = pl.pallas_call(
        functools.partial(up_first_kernel, count),
        in_specs=[SMEM, VMEM] + [HBM] * 4 + [VMEM] * count,
        out_specs=[VMEM] * 3,
        out_shape=[
            jax.ShapeDtypeStruct((4, rows, width), jnp.float32),
            jax.ShapeDtypeStruct((rows, HD), jnp.float32),
            jax.ShapeDtypeStruct(weights, jnp.bfloat16),
        ],
        scratch_shapes=[
            pltpu.VMEM((count,) + weights, jnp.bfloat16),
            pltpu.SemaphoreType.DMA((count + 1, 4)),
        ],
        compiler_params=PARAMS,
        cost_estimate=cost(8 * count * rows * depth * width, 8 * count * depth * width),
    )(places, gain, *sources, *early)
    return pl.pallas_call(
        up_last_kernel,
        in_specs=[SMEM] + [VMEM] * 5,
        out_specs=VMEM,
        out_shape=jax.ShapeDtypeStruct((rows, 2 * width), jnp.bfloat16),
        compiler_params=PARAMS,
        cost_estimate=cost(8 * rows * depth * width, 8 * depth * width, 2 * rows * width),
    )(places, gain, late, *sums)


def expert_outputs(blocks, places, own, other, shape):
    (rows, width), cols = blocks[0].shape, own.shape[1]
    own = pltpu.with_memory_space_constraint(own, pltpu.HBM)
    other = pltpu.with_memory_space_constraint(other, pltpu.HBM)
    *early, late = blocks
    count = len(early)
    weights = (2, width // 2, cols)
    sums = pl.pallas_call(
        functools.partial(down_first_kernel, count),
        in_specs=[SMEM, HBM, HBM] + [VMEM] * count,
        out_specs=[VMEM] * 2,
        out_shape=[
            jax.ShapeDtypeStruct((rows, cols), jnp.float32),
            jax.ShapeDtypeStruct(weights, jnp.bfloat16),
        ],
        scratch_shapes=[
            pltpu.VMEM((count,) + weights, jnp.bfloat16),
            pltpu.SemaphoreType.DMA((count + 1, 2)),
        ],
        compiler_params=PARAMS,
        cost_estimate=cost(2 * count * rows * width * cols, 2 * count * width * (rows + cols)),
    )(places, own, other, *early)
    return pl.pallas_call(
        down_last_kernel,
        in_specs=[VMEM] * 3,
        out_specs=VMEM,
        out_shape=jax.ShapeDtypeStruct(shape, jnp.bfloat16),
        scratch_shapes=[pltpu.VMEM((rows, cols), jnp.float32)],
        compiler_params=PARAMS,
        cost_estimate=cost(2 * rows * width * cols, 2 * width * (rows + cols)),
    )(late, *sums)


def around(block, axis):
    size = lax.axis_size(axis)
    before, after, blocks = block, block, [block]
    for distance in range(1, size // 2 + 1):
        before = shift(before, axis, 1)
        blocks.append(before)
        if distance < size - distance:
            after = shift(after, axis, size - 1)
            blocks.append(after)
    return blocks


def combine_kernel(picker_ref, parts_ref, out_ref, total_ref):
    chips, experts, capacity, _ = parts_ref.shape
    for expert in range(experts):
        total = parts_ref[0, expert].astype(jnp.float32)
        for chip in range(1, chips):
            total = total + parts_ref[chip, expert].astype(jnp.float32)
        total_ref[pl.ds(expert * capacity, capacity)] = total
    picked = lax.dot_general(
        picker_ref[...],
        total_ref[...],
        (((0,), (0,)), ((), ())),
        precision=lax.Precision.HIGHEST,
        preferred_element_type=jnp.float32,
    )
    out_ref[...] = picked.astype(out_ref.dtype)


def combined(picker, parts):
    (slots, rows), cols = picker.shape, parts.shape[3]
    return pl.pallas_call(
        combine_kernel,
        in_specs=[VMEM] * 2,
        out_specs=VMEM,
        out_shape=jax.ShapeDtypeStruct((rows, cols), jnp.bfloat16),
        scratch_shapes=[pltpu.VMEM((slots, cols), jnp.float32)],
        compiler_params=PARAMS,
    )(picker, parts)


def body(
    queries,
    key_cache,
    value_cache,
    new_key,
    new_value,
    lengths,
    residual,
    norm_gain,
    routes,
    route_weights,
    w_gate_up,
    w_down,
):
    n_x, n_tp, n_exp = lax.axis_size("x"), lax.axis_size("tp"), lax.axis_size("exp")

    attn_out, packed, picker = attend_and_pack(
        lengths,
        routes.T,
        route_weights.T,
        [queries, new_key, new_value, residual, key_cache, value_cache],
        n_x,
    )
    _, _, capacity, part = packed.shape
    packed = packed.reshape(n_x * n_exp, capacity, part)
    packed, w_gate_up, w_down = lax.optimization_barrier((packed, w_gate_up, w_down))
    gate_own, up_own, down_own = w_gate_up[0, :, 0], w_gate_up[0, :, 1], w_down[0]
    gate_other, up_other, down_other = (
        shift(weights, "core", 1) for weights in (gate_own, up_own, down_own)
    )
    arrived = lax.all_to_all(packed, ("x", "exp"), split_axis=0, concat_axis=0, tiled=True)
    arrived = arrived.reshape(n_x * n_exp * capacity, part)

    distance = jnp.array([0, -1, 1, -2, 2, -3, 3, 4], jnp.int32)
    places = (lax.axis_index("tp") + distance) % n_tp
    blocks = around(arrived, "tp")
    sources = (gate_own, up_own, gate_other, up_other)
    units = expert_units(blocks, places, norm_gain[None, :], sources)
    blocks = around(units, "tp")
    shape = (n_x * n_exp, capacity, part)
    partial = expert_outputs(blocks, places, down_own, down_other, shape)

    returned = lax.all_to_all(partial, ("x", "exp"), split_axis=0, concat_axis=0, tiled=True)
    moe_out = combined(picker, returned.reshape(n_x, n_exp, capacity, part))
    return (attn_out, moe_out)


def solution(mesh):
    sizes = mesh.shape
    cores = 2
    chips = Mesh(
        mesh.devices.reshape(sizes["attn"] // cores, cores, sizes["tp"], sizes["exp"]),
        ("x", "core", "tp", "exp"),
    )
    rows = ("x", "core", "exp")
    return jax.shard_map(
        body,
        mesh=chips,
        in_specs=(
            P(rows, "tp"),
            P(rows, "tp", None, None),
            P(rows, "tp", None, None),
            P(rows, "tp"),
            P(rows, "tp"),
            P(rows),
            P(rows, "tp"),
            P(),
            P(rows, None),
            P(rows, None),
            P("exp", None, None, ("x", "core", "tp")),
            P("exp", ("x", "core"), "tp"),
        ),
        out_specs=(P(rows, "tp"), P(rows, "tp")),
        check_vma=False,
    )
```
